512 devices in a mesh: row: 32 (over y_lo, z), col: 16 (over y_hi, x, core).
Axes of the slice: x: 4, y: 4 (y_hi: 2, y_lo: 2; y = y_hi * 2 + y_lo), z: 16, core: 2. Of those that a mesh axis runs over, the one named last changes fastest.
Arguments:
- amplitudes: float32 [1280, 180224], P('row', 'col'), may hold values from -6 to 6
- integrals: float32 [768, 16, 32, 352], P(None, 'col', 'row'), may hold values from -0.013671875 to 0.013671875
Outputs:
- ladder: float32 [768, 1280], P('row', 'col')
The draws below stay inside these ranges and needn't reach their ends.
All inputs are finite; a program needn't handle non-finite values.
Results may differ from the reference program's by a relative error of at most 0.000084.
Values sent between devices are 32-bit elements; how exact they have to be, the bound alone decides.
A program may use at most 64 MiB of HBM per device.

```python
import jax
import jax.numpy as jnp
from jax import lax

SLAB = 768
OPAIRS = 1280
VPAIRS = 180224
KB = 352
N_ROW = 32
N_COL = 16


def shard_levels(key, extent, pieces, low, top_value):
    gain, own = 1.0, jax.random.fold_in(key, 6)
    for position, parts in pieces:
        draws = jnp.exp(jax.random.uniform(jax.random.fold_in(own, position), (parts,), jnp.float32, low / len(pieces), top_value / len(pieces)))
        gain = gain * jnp.repeat(draws, extent[position] // parts).reshape([-1 if axis == position else 1 for axis in range(len(extent))])
    return gain


def gaussian(own_key, extent, scale, bound, pieces=(), held_as=jnp.bfloat16):
    drawn = jax.random.normal(own_key, extent, jnp.float32) * scale
    if len(pieces) > 0:
        drawn = shard_levels(own_key, extent, pieces, -0.22, 0.18) * drawn
    return jnp.clip(drawn, min=-bound, max=bound).astype(held_as)


def setup_inputs(seed: int = 0) -> dict:
    arg_keys = jax.random.split(jax.random.key(seed), 3)
    amplitudes = gaussian(arg_keys[0], (OPAIRS, VPAIRS), 1.0, 6.0, ((0, 32), (1, 16)), jnp.float32)
    integrals = gaussian(arg_keys[1], (SLAB, N_COL, N_ROW, KB), VPAIRS ** -0.5, 0.013671875, ((1, 16), (2, 32)), jnp.float32)
    return {"amplitudes": amplitudes, "integrals": integrals}


def reference(amplitudes, integrals):
    flattened = integrals.reshape(integrals.shape[0], -1)
    return lax.dot_general(flattened, amplitudes, (((1,), (1,)), ((), ())), precision=lax.Precision.HIGHEST, preferred_element_type=jnp.float32)
```

```python
import jax
import jax.numpy as jnp
from jax import lax
from jax.experimental import pallas as pl
from jax.experimental.pallas import tpu as pltpu
from jax.sharding import PartitionSpec as P

MESH = pl.DeviceIdType.MESH
ROUNDS = 5
F32 = jnp.float32
BF16 = jnp.bfloat16


def wait_for(ref, sem):
    pltpu.make_async_copy(ref, ref, sem).wait()


def kernel(
    amp_hbm, int_hbm, out_ref,
    amp, ints, hi, lo, send_a, send_b, recv_a, recv_b,
    part, plane, near_out, near_in, total, far_out, far_in,
    load_sem, int_sem, send_sem, recv_sem, plane_send, plane_recv, near_send, near_recv, far_send, far_recv,
):
    row, col = lax.axis_index("row"), lax.axis_index("col")
    half, z = row // 16, row % 16
    z_hi, z_lo = z // 4, z % 4
    chip, core = col // 2, col % 2
    parity = (row // 2) % 2
    slot = (row // 4) * 2 + row % 2
    place = half * 8 + chip
    target = chip * 2 + parity
    mine = parity == core

    load_amp = pltpu.make_async_copy(amp_hbm, amp, load_sem.at[0])
    load_amp.start()
    load_int = pltpu.make_async_copy(int_hbm, ints.at[core], load_sem.at[1])
    load_int.start()

    def plane_peer(d):
        other = (place + d) % 16
        return other // 8, other % 8, ((other // 8) * 16 + z, (other % 8) * 2 + core)

    def near_peer(d):
        other = (z_lo + d) % 4
        return other, (half * 16 + z_hi * 4 + other, col)

    def far_peer(d):
        other = (z_hi + d) % 4
        return other, (half * 16 + other * 4 + z_lo, col)

    barrier = pltpu.get_barrier_semaphore()

    def greet(device):
        pl.semaphore_signal(barrier, inc=1, device_id=device, device_id_type=MESH)

    def greet_source(t, carry):
        source = (t // 4) * 4 + core * 2 + (t // 2) % 2
        source_col = chip * 2 + t % 2

        @pl.when(jnp.logical_or(source != row, source_col != col))
        def _():
            greet((source, source_col))

        return carry

    lax.fori_loop(0, 32, greet_source, 0)

    def greet_plane(d, carry):
        greet(plane_peer(16 - d)[2])
        return carry

    lax.fori_loop(1, 16, greet_plane, 0)
    for d in range(1, 4):
        greet(near_peer(4 - d)[1])
        greet(far_peer(4 - d)[1])
    greet((row, chip * 2 + 1 - core))

    load_amp.wait()

    def pack(g, carry):
        lane = lax.broadcasted_iota(jnp.int32, (40, 128), 1)
        lane8 = lax.broadcasted_iota(jnp.int32, (8, 128), 1)

        def load(t):
            return amp[:, pl.ds(pl.multiple_of(g * 1408 + t * 128, 128), 128)]

        for j in range(4):
            first, shift = (352 * j) // 128, (352 * j) % 128
            tiles = []
            for n in range(3):
                tile = load(first + n)
                if shift > 0:
                    tile = pltpu.roll(tile, 128 - shift, 1)
                    if first + n + 1 <= 10:
                        after = pltpu.roll(load(first + n + 1), 128 - shift, 1)
                        tile = jnp.where(lane < 128 - shift, tile, after)
                tiles.append(tile)
            dest = g * 4 + j
            for i in range(4):
                send_a[i, dest, 0] = tiles[0][8 * i:8 * i + 8]
                send_a[i, dest, 1] = tiles[1][8 * i:8 * i + 8]
                spare = pltpu.roll(tiles[2][32:40], 96 - 32 * i, 1) if i < 3 else jnp.zeros((8, 128), F32)
                send_a[i, dest, 2] = jnp.where(lane8 < 96, tiles[2][8 * i:8 * i + 8], spare)
            send_b[dest, 0] = tiles[0][32:40]
            send_b[dest, 1] = tiles[1][32:40]
        return carry

    lax.fori_loop(0, 8, pack, 0)
    load_int.wait()

    copies = jnp.where(mine, 31, 32)
    pl.semaphore_wait(barrier, copies + 15 + 3 + 3 + 1)

    sibling = pltpu.make_async_remote_copy(
        ints.at[core], ints.at[core], int_sem.at[0], int_sem.at[1],
        device_id=(row, chip * 2 + 1 - core), device_id_type=MESH,
    )
    sibling.start()

    def outgoing(i):
        return send_a.at[i] if i < 4 else send_b

    def incoming(i):
        return recv_a.at[i] if i < 4 else recv_b

    def send_round(i):
        src, dst = outgoing(i), incoming(i).at[core, slot]

        def send(t, carry):
            other = (row + t) % 32
            pltpu.make_async_remote_copy(
                src.at[other], dst, send_sem.at[i], recv_sem.at[i],
                device_id=(other, target), device_id_type=MESH,
            ).start()
            return carry

        lax.fori_loop(1, 32, send, 0)

        @pl.when(mine)
        def _():
            pltpu.make_async_copy(src.at[row], dst, recv_sem.at[i]).start()

        @pl.when(jnp.logical_not(mine))
        def _():
            pltpu.make_async_remote_copy(
                src.at[row], dst, send_sem.at[i], recv_sem.at[i],
                device_id=(row, target), device_id_type=MESH,
            ).start()

    send_round(0)
    send_round(1)

    sibling.wait()
    for c in range(2):
        whole = ints[c]
        upper = whole.astype(BF16)
        hi[384 * c:384 * c + 352] = upper
        lo[384 * c:384 * c + 352] = (whole - upper.astype(F32)).astype(BF16)
        hi[384 * c + 352:384 * c + 384] = jnp.zeros((32, 768), BF16)
        lo[384 * c + 352:384 * c + 384] = jnp.zeros((32, 768), BF16)

    def gathered(i):
        parts = []
        for c in range(2):
            if i < 4:
                parts += [recv_a[i, c, :, n].reshape(128, 128) for n in range(3)]
            else:
                lane = lax.broadcasted_iota(jnp.int32, (128, 128), 1)
                last = jnp.zeros((128, 128), F32)
                for g in range(3):
                    moved = pltpu.roll(recv_a[g, c, :, 2].reshape(128, 128), 32 + 32 * g, 1)
                    last = jnp.where(jnp.logical_and(lane >= 32 * g, lane < 32 * g + 32), moved, last)
                parts += [recv_b[c, :, n].reshape(128, 128) for n in range(2)] + [last]
        return jnp.concatenate(parts, axis=1)

    def product(i):
        left = gathered(i)
        upper = left.astype(BF16)
        lower = (left - upper.astype(F32)).astype(BF16)
        for h in range(2):
            lanes = slice(384 * h, 384 * h + 384)
            summed = jnp.dot(upper, lo[:, lanes], preferred_element_type=F32)
            summed += jnp.dot(lower, hi[:, lanes], preferred_element_type=F32)
            summed += jnp.dot(upper, hi[:, lanes], preferred_element_type=F32)
            part[i, h] = summed.reshape(8, 16, 384)

    def send_plane(i):
        def send(d, carry):
            other_half, other_chip, device = plane_peer(d)
            pltpu.make_async_remote_copy(
                part.at[i, other_half, other_chip], plane.at[i, d - 1], plane_send.at[i], plane_recv.at[i],
                device_id=device, device_id_type=MESH,
            ).start()
            return carry

        lax.fori_loop(1, 16, send, 0)

    def sum_plane(i):
        wait_for(plane.at[i], plane_recv.at[i])
        summed = part[i, half, chip]
        for d in range(15):
            summed = summed + plane[i, d]
        lane = lax.broadcasted_iota(jnp.int32, (16, 128), 1)
        for low in range(4):
            spread = jnp.zeros((16, 128), F32)
            for high in range(4):
                start = 24 * (4 * high + low)
                done = 0
                while done < 24:
                    tile, offset = (start + done) // 128, (start + done) % 128
                    count = min(24 - done, 128 - offset)
                    to = 32 * high + done
                    moved = summed[:, 128 * tile:128 * tile + 128]
                    if (to - offset) % 128:
                        moved = pltpu.roll(moved, (to - offset) % 128, 1)
                    spread = jnp.where(jnp.logical_and(lane >= to, lane < to + count), moved, spread)
                    done += count
            near_out[i, low] = spread
        for d in range(1, 4):
            other, device = near_peer(d)
            pltpu.make_async_remote_copy(
                near_out.at[i, other], near_in.at[i, d - 1], near_send.at[i, d - 1], near_recv.at[i, d - 1],
                device_id=device, device_id_type=MESH,
            ).start()

    def sum_near(i):
        summed = near_out[i, z_lo]
        for d in range(1, 4):
            wait_for(near_in.at[i, d - 1], near_recv.at[i, d - 1])
            summed = summed + near_in[i, d - 1]
        total[8 * i:8 * i + 8] = summed[0:8]
        total[40 + 8 * i:48 + 8 * i] = summed[8:16]

    total[80:128] = jnp.zeros((48, 128), F32)
    for i in range(ROUNDS):
        wait_for(incoming(i), recv_sem.at[i])
        if i + 2 < ROUNDS:
            send_round(i + 2)
        product(i)
        send_plane(i)
        if i >= 1:
            sum_plane(i - 1)
        if i >= 2:
            sum_near(i - 2)
    sum_near(ROUNDS - 2)
    sum_plane(ROUNDS - 1)
    sum_near(ROUNDS - 1)

    far_out[...] = total[...].T.reshape(4, 32, 128)
    for d in range(1, 4):
        other, device = far_peer(d)
        pltpu.make_async_remote_copy(
            far_out.at[other, pl.ds(0, 24)], far_in.at[d - 1], far_send.at[d - 1], far_recv.at[d - 1],
            device_id=device, device_id_type=MESH,
        ).start()
    summed = far_out[z_hi, 0:24]
    for d in range(1, 4):
        wait_for(far_in.at[d - 1], far_recv.at[d - 1])
        summed = summed + far_in[d - 1]
    out_ref[...] = summed[:, 0:80]

    for i in range(ROUNDS):
        @pl.when(mine)
        def _():
            wait_for(outgoing(i).at[pl.ds(0, 31)], send_sem.at[i])

        @pl.when(jnp.logical_not(mine))
        def _():
            wait_for(outgoing(i), send_sem.at[i])

        wait_for(plane.at[i], plane_send.at[i])
        for d in range(3):
            wait_for(near_in.at[i, d], near_send.at[i, d])
    for d in range(3):
        wait_for(far_in.at[d], far_send.at[d])


def per_device(amplitudes, integrals):
    flat = integrals.reshape(768, 352).T
    dma = pltpu.SemaphoreType.DMA
    return pl.pallas_call(
        kernel,
        out_shape=jax.ShapeDtypeStruct((24, 80), F32),
        in_specs=[pl.BlockSpec(memory_space=pl.ANY)] * 2,
        out_specs=pl.BlockSpec(memory_space=pltpu.VMEM),
        scratch_shapes=[
            pltpu.VMEM((40, 11264), F32),
            pltpu.VMEM((2, 352, 768), F32),
            pltpu.VMEM((768, 768), BF16),
            pltpu.VMEM((768, 768), BF16),
            pltpu.VMEM((4, 32, 3, 8, 128), F32),
            pltpu.VMEM((32, 2, 8, 128), F32),
            pltpu.VMEM((4, 2, 16, 3, 8, 128), F32),
            pltpu.VMEM((2, 16, 2, 8, 128), F32),
            pltpu.VMEM((ROUNDS, 2, 8, 16, 384), F32),
            pltpu.VMEM((ROUNDS, 15, 16, 384), F32),
            pltpu.VMEM((ROUNDS, 4, 16, 128), F32),
            pltpu.VMEM((ROUNDS, 3, 16, 128), F32),
            pltpu.VMEM((128, 128), F32),
            pltpu.VMEM((4, 32, 128), F32),
            pltpu.VMEM((3, 24, 128), F32),
            dma((2,)),
            dma((2,)),
            dma((ROUNDS,)),
            dma((ROUNDS,)),
            dma((ROUNDS,)),
            dma((ROUNDS,)),
            dma((ROUNDS, 3)),
            dma((ROUNDS, 3)),
            dma((3,)),
            dma((3,)),
        ],
        compiler_params=pltpu.CompilerParams(
            collective_id=0, has_side_effects=True, vmem_limit_bytes=40 << 20
        ),
    )(amplitudes, flat)


def solution(mesh):
    return jax.shard_map(
        per_device,
        mesh=mesh,
        in_specs=(P("row", "col"), P(None, "col", "row", None)),
        out_specs=P("row", "col"),
        check_vma=False,
    )
```

```python
import jax
import jax.numpy as jnp
from jax import lax
from jax.experimental import pallas as pl
from jax.experimental.pallas import tpu as pltpu
from jax.sharding import PartitionSpec as P

MESH = pl.DeviceIdType.MESH
ROUNDS = 6
F32 = jnp.float32
BF16 = jnp.bfloat16


def wait_for(ref, sem):
    pltpu.make_async_copy(ref, ref, sem).wait()


def kernel(
    amp_hbm, int_hbm, out_ref,
    amp, ints, hi, lo, send_a, send_b, recv_a, recv_b,
    part_a, part_b, plane_a, plane_b, near_out_a, near_out_b, near_in_a, near_in_b, total, turned, far_out, far_in, last_in,
    load_sem, int_sem, send_sem, recv_sem, plane_send, plane_recv, near_send, near_recv, far_send, far_recv,
    last_send, last_recv,
):
    row, col = lax.axis_index("row"), lax.axis_index("col")
    half, z = row // 16, row % 16
    z_hi, z_lo = z // 4, z % 4
    chip, core = col // 2, col % 2
    parity = (row // 2) % 2
    slot = (row // 4) * 2 + row % 2
    place = half * 8 + chip
    target = chip * 2 + parity
    mine = parity == core

    load_amp = pltpu.make_async_copy(amp_hbm, amp, load_sem.at[0])
    load_amp.start()
    load_int = pltpu.make_async_copy(int_hbm, ints.at[core], load_sem.at[1])
    load_int.start()

    def plane_peer(d):
        other = (place + d) % 16
        return other // 8, other % 8, ((other // 8) * 16 + z, (other % 8) * 2 + core)

    def near_peer(d):
        other = (z_lo + d) % 4
        return other, (half * 16 + z_hi * 4 + other, col)

    def far_peer(d):
        other = (z_hi + d) % 4
        return other, (half * 16 + other * 4 + z_lo, col)

    def z_peer(d):
        other = (z + d) % 16
        return other, (half * 16 + other, col)

    barrier = pltpu.get_barrier_semaphore()

    def greet(device):
        pl.semaphore_signal(barrier, inc=1, device_id=device, device_id_type=MESH)

    def greet_source(t, carry):
        source = (t // 4) * 4 + core * 2 + (t // 2) % 2
        source_col = chip * 2 + t % 2

        @pl.when(jnp.logical_or(source != row, source_col != col))
        def _():
            greet((source, source_col))

        return carry

    lax.fori_loop(0, 32, greet_source, 0)

    def greet_plane(d, carry):
        greet(plane_peer(16 - d)[2])
        return carry

    def greet_z(d, carry):
        greet(z_peer(16 - d)[1])
        return carry

    lax.fori_loop(1, 16, greet_plane, 0)
    lax.fori_loop(1, 16, greet_z, 0)
    greet((row, chip * 2 + 1 - core))

    load_amp.wait()

    def pack(g, carry):
        lane = lax.broadcasted_iota(jnp.int32, (40, 128), 1)
        lane8 = lax.broadcasted_iota(jnp.int32, (8, 128), 1)
        sub8 = lax.broadcasted_iota(jnp.int32, (8, 128), 0)

        def load(t):
            return amp[:, pl.ds(pl.multiple_of(g * 1408 + t * 128, 128), 128)]

        for j in range(4):
            first, shift = (352 * j) // 128, (352 * j) % 128
            tiles = []
            for n in range(3):
                tile = load(first + n)
                if shift > 0:
                    tile = pltpu.roll(tile, 128 - shift, 1)
                    if first + n + 1 <= 10:
                        after = pltpu.roll(load(first + n + 1), 128 - shift, 1)
                        tile = jnp.where(lane < 128 - shift, tile, after)
                tiles.append(tile)
            dest = g * 4 + j
            for i in range(4):
                send_a[i, dest, 0] = tiles[0][8 * i:8 * i + 8]
                send_a[i, dest, 1] = tiles[1][8 * i:8 * i + 8]
                spare = pltpu.roll(tiles[2][32:40], 96 - 32 * i, 1) if i < 3 else jnp.zeros((8, 128), F32)
                send_a[i, dest, 2] = jnp.where(lane8 < 96, tiles[2][8 * i:8 * i + 8], spare)
            first8, second8 = tiles[0][32:40], tiles[1][32:40]
            send_b[0, dest] = jnp.where(sub8 < 4, first8, pltpu.roll(second8, 4, 0))
            send_b[1, dest] = jnp.where(sub8 < 4, pltpu.roll(first8, 4, 0), second8)
        return carry

    lax.fori_loop(0, 8, pack, 0)
    load_int.wait()

    copies = jnp.where(mine, 31, 32)
    pl.semaphore_wait(barrier, copies + 15 + 15 + 1)

    sibling = pltpu.make_async_remote_copy(
        ints.at[core], ints.at[core], int_sem.at[0], int_sem.at[1],
        device_id=(row, chip * 2 + 1 - core), device_id_type=MESH,
    )
    sibling.start()

    def outgoing(i):
        return send_a.at[i] if i < 4 else send_b.at[i - 4]

    def incoming(i):
        return recv_a.at[i] if i < 4 else recv_b.at[i - 4]

    def part(i):
        return part_a.at[i] if i < 4 else part_b.at[i - 4]

    def plane(i):
        return plane_a.at[i] if i < 4 else plane_b.at[i - 4]

    def near_out(i):
        return near_out_a.at[i] if i < 4 else near_out_b.at[i - 4]

    def near_in(i):
        return near_in_a.at[i] if i < 4 else near_in_b

    def send_round(i):
        src, dst = outgoing(i), incoming(i).at[core, slot]

        def send(t, carry):
            other = (row + t) % 32
            pltpu.make_async_remote_copy(
                src.at[other], dst, send_sem.at[i], recv_sem.at[i],
                device_id=(other, target), device_id_type=MESH,
            ).start()
            return carry

        lax.fori_loop(1, 32, send, 0)

        @pl.when(mine)
        def _():
            pltpu.make_async_copy(src.at[row], dst, recv_sem.at[i]).start()

        @pl.when(jnp.logical_not(mine))
        def _():
            pltpu.make_async_remote_copy(
                src.at[row], dst, send_sem.at[i], recv_sem.at[i],
                device_id=(row, target), device_id_type=MESH,
            ).start()

    send_round(0)
    send_round(1)

    sibling.wait()
    for c in range(2):
        whole = ints[c]
        upper = whole.astype(BF16)
        hi[384 * c:384 * c + 352] = upper
        lo[384 * c:384 * c + 352] = (whole - upper.astype(F32)).astype(BF16)
        hi[384 * c + 352:384 * c + 384] = jnp.zeros((32, 768), BF16)
        lo[384 * c + 352:384 * c + 384] = jnp.zeros((32, 768), BF16)

    def gathered(i):
        if i < 4:
            return jnp.concatenate(
                [recv_a[i, c, :, n].reshape(128, 128) for c in range(2) for n in range(3)], axis=1
            )
        sub = lax.broadcasted_iota(jnp.int32, (64, 128), 0) % 8
        lane = lax.broadcasted_iota(jnp.int32, (64, 128), 1)

        def evens_odds(ref):
            whole = ref.reshape(8, 2, 8, 128)
            return whole[:, 0].reshape(64, 128), whole[:, 1].reshape(64, 128)

        def upper_rows(even, odd):
            return jnp.where(sub < 4, even, pltpu.roll(odd, 4, 0))

        def lower_rows(even, odd):
            return jnp.where(sub < 4, pltpu.roll(even, 60, 0), odd)

        parts = []
        for c in range(2):
            even, odd = evens_odds(recv_b[i - 4, c])
            parts += [upper_rows(even, odd), lower_rows(even, odd)]
            last = jnp.zeros((64, 128), F32)
            for g in range(3):
                even, odd = evens_odds(recv_a[g, c, :, 2])
                merged = upper_rows(even, odd) if i == 4 else lower_rows(even, odd)
                moved = pltpu.roll(merged, 32 + 32 * g, 1)
                last = jnp.where(jnp.logical_and(lane >= 32 * g, lane < 32 * g + 32), moved, last)
            parts.append(last)
        return jnp.concatenate(parts, axis=1)

    def product(i):
        left = gathered(i)
        upper = left.astype(BF16)
        lower = (left - upper.astype(F32)).astype(BF16)
        for h in range(2):
            lanes = slice(384 * h, 384 * h + 384)
            summed = jnp.dot(upper, lo[:, lanes], preferred_element_type=F32)
            summed += jnp.dot(lower, hi[:, lanes], preferred_element_type=F32)
            summed += jnp.dot(upper, hi[:, lanes], preferred_element_type=F32)
            part(i)[h] = summed.reshape(8, 16 if i < 4 else 8, 384)

    def send_plane(i):
        def send(d, carry):
            other_half, other_chip, device = plane_peer(d)
            pltpu.make_async_remote_copy(
                part(i).at[other_half, other_chip], plane(i).at[d - 1], plane_send.at[i], plane_recv.at[i],
                device_id=device, device_id_type=MESH,
            ).start()
            return carry

        lax.fori_loop(1, 16, send, 0)

    def sum_plane(i):
        wait_for(plane(i), plane_recv.at[i])
        summed = part(i)[half, chip]
        for d in range(15):
            summed = summed + plane(i)[d]
        rows = summed.shape[0]
        lane = lax.broadcasted_iota(jnp.int32, (rows, 128), 1)
        for low in range(4):
            spread = jnp.zeros((rows, 128), F32)
            for high in range(4):
                start = 24 * (4 * high + low)
                done = 0
                while done < 24:
                    tile, offset = (start + done) // 128, (start + done) % 128
                    count = min(24 - done, 128 - offset)
                    to = 32 * high + done
                    moved = summed[:, 128 * tile:128 * tile + 128]
                    if (to - offset) % 128:
                        moved = pltpu.roll(moved, (to - offset) % 128, 1)
                    spread = jnp.where(jnp.logical_and(lane >= to, lane < to + count), moved, spread)
                    done += count
            near_out(i)[low] = spread

    def send_near(i):
        for d in range(1, 4):
            other, device = near_peer(d)
            pltpu.make_async_remote_copy(
                near_out(i).at[other], near_in(i).at[d - 1], near_send.at[i, d - 1], near_recv.at[i, d - 1],
                device_id=device, device_id_type=MESH,
            ).start()

    def sum_near(i):
        summed = near_out(i)[z_lo]
        for d in range(1, 4):
            wait_for(near_in(i).at[d - 1], near_recv.at[i, d - 1])
            summed = summed + near_in(i)[d - 1]
        if i < 4:
            total[8 * i:8 * i + 8] = summed[0:8]
            total[40 + 8 * i:48 + 8 * i] = summed[8:16]
        else:
            sub = lax.broadcasted_iota(jnp.int32, (8, 128), 0)
            total[32:40] = jnp.where(sub < 4, summed, 0.0)
            total[72:80] = jnp.where(sub < 4, pltpu.roll(summed, 4, 0), 0.0)

    total[80:128] = jnp.zeros((48, 128), F32)
    for i in range(ROUNDS):
        wait_for(incoming(i), recv_sem.at[i])
        if i + 2 < ROUNDS:
            send_round(i + 2)
        product(i)
        send_plane(i)
        if i >= 1:
            sum_plane(i - 1)
            send_near(i - 1)
        if i >= 2:
            sum_near(i - 2)
    sum_near(ROUNDS - 2)

    far_out[...] = total[...].T.reshape(4, 32, 128)
    for d in range(1, 4):
        other, device = far_peer(d)
        pltpu.make_async_remote_copy(
            far_out.at[other, pl.ds(0, 24)], far_in.at[d - 1], far_send.at[d - 1], far_recv.at[d - 1],
            device_id=device, device_id_type=MESH,
        ).start()

    sum_plane(ROUNDS - 1)

    def send_last(d, carry):
        other, device = z_peer(d)
        pltpu.make_async_remote_copy(
            near_out_b.at[1, other % 4], last_in.at[d - 1], last_send, last_recv,
            device_id=device, device_id_type=MESH,
        ).start()
        return carry

    lax.fori_loop(1, 16, send_last, 0)
    summed = far_out[z_hi, 0:24]
    for d in range(1, 4):
        wait_for(far_in.at[d - 1], far_recv.at[d - 1])
        summed = summed + far_in[d - 1]

    wait_for(last_in, last_recv)
    last = near_out_b[1, z_lo]
    for d in range(15):
        last = last + last_in[d]
    sub = lax.broadcasted_iota(jnp.int32, (8, 128), 0)
    total[0:32] = jnp.zeros((32, 128), F32)
    total[32:40] = jnp.where(sub < 4, 0.0, pltpu.roll(last, 4, 0))
    total[40:72] = jnp.zeros((32, 128), F32)
    total[72:80] = jnp.where(sub < 4, 0.0, last)
    turned[...] = total[...].T.reshape(4, 32, 128)
    out_ref[...] = (summed + turned[z_hi, 0:24])[:, 0:80]

    for i in range(ROUNDS):
        @pl.when(mine)
        def _():
            wait_for(outgoing(i).at[pl.ds(0, 31)], send_sem.at[i])

        @pl.when(jnp.logical_not(mine))
        def _():
            wait_for(outgoing(i), send_sem.at[i])

        wait_for(plane(i), plane_send.at[i])
        if i < ROUNDS - 1:
            for d in range(3):
                wait_for(near_in(i).at[d], near_send.at[i, d])
    for d in range(3):
        wait_for(far_in.at[d], far_send.at[d])
    wait_for(last_in, last_send)


def per_device(amplitudes, integrals):
    flat = integrals.reshape(768, 352).T
    dma = pltpu.SemaphoreType.DMA
    return pl.pallas_call(
        kernel,
        out_shape=jax.ShapeDtypeStruct((24, 80), F32),
        in_specs=[pl.BlockSpec(memory_space=pl.ANY)] * 2,
        out_specs=pl.BlockSpec(memory_space=pltpu.VMEM),
        scratch_shapes=[
            pltpu.VMEM((40, 11264), F32),
            pltpu.VMEM((2, 352, 768), F32),
            pltpu.VMEM((768, 768), BF16),
            pltpu.VMEM((768, 768), BF16),
            pltpu.VMEM((4, 32, 3, 8, 128), F32),
            pltpu.VMEM((2, 32, 8, 128), F32),
            pltpu.VMEM((4, 2, 16, 3, 8, 128), F32),
            pltpu.VMEM((2, 2, 16, 8, 128), F32),
            pltpu.VMEM((4, 2, 8, 16, 384), F32),
            pltpu.VMEM((2, 2, 8, 8, 384), F32),
            pltpu.VMEM((4, 15, 16, 384), F32),
            pltpu.VMEM((2, 15, 8, 384), F32),
            pltpu.VMEM((4, 4, 16, 128), F32),
            pltpu.VMEM((2, 4, 8, 128), F32),
            pltpu.VMEM((4, 3, 16, 128), F32),
            pltpu.VMEM((3, 8, 128), F32),
            pltpu.VMEM((128, 128), F32),
            pltpu.VMEM((4, 32, 128), F32),
            pltpu.VMEM((4, 32, 128), F32),
            pltpu.VMEM((3, 24, 128), F32),
            pltpu.VMEM((15, 8, 128), F32),
            dma((2,)),
            dma((2,)),
            dma((ROUNDS,)),
            dma((ROUNDS,)),
            dma((ROUNDS,)),
            dma((ROUNDS,)),
            dma((ROUNDS, 3)),
            dma((ROUNDS, 3)),
            dma((3,)),
            dma((3,)),
            dma,
            dma,
        ],
        compiler_params=pltpu.CompilerParams(
            collective_id=0, has_side_effects=True, vmem_limit_bytes=60 << 20
        ),
    )(amplitudes, flat)


def solution(mesh):
    return jax.shard_map(
        per_device,
        mesh=mesh,
        in_specs=(P("row", "col"), P(None, "col", "row", None)),
        out_specs=P("row", "col"),
        check_vma=False,
    )
```

```python
import jax
import jax.numpy as jnp
from jax import lax
from jax.experimental import pallas as pl
from jax.experimental.pallas import tpu as pltpu
from jax.sharding import PartitionSpec as P

MESH = pl.DeviceIdType.MESH
ROUNDS = 6
F32 = jnp.float32
BF16 = jnp.bfloat16


def wait_for(ref, sem):
    pltpu.make_async_copy(ref, ref, sem).wait()


def kernel(
    amp_hbm, int_hbm, out_ref,
    amp, ints, hi, lo, send_a, send_b, recv_a, recv_b,
    part_a, part_b, plane_a, plane_b, near_out_a, near_out_b, near_in, total, turned, far_out, far_in, last_in,
    load_sem, int_sem, send_sem, recv_sem, plane_send, plane_recv, near_send, near_recv, far_send, far_recv,
    last_send, last_recv,
):
    row, col = lax.axis_index("row"), lax.axis_index("col")
    half, z = row // 16, row % 16
    z_hi, z_lo = z // 4, z % 4
    chip, core = col // 2, col % 2
    parity = (row // 2) % 2
    slot = (row // 4) * 2 + row % 2
    place = half * 8 + chip
    target = chip * 2 + parity
    mine = parity == core

    load_amp = pltpu.make_async_copy(amp_hbm, amp, load_sem.at[0])
    load_amp.start()
    load_int = pltpu.make_async_copy(int_hbm, ints.at[core], load_sem.at[1])
    load_int.start()

    def plane_peer(d):
        other = (place + d) % 16
        return other // 8, other % 8, ((other // 8) * 16 + z, (other % 8) * 2 + core)

    def near_peer(d):
        other = (z_lo + d) % 4
        return other, (half * 16 + z_hi * 4 + other, col)

    def far_peer(d):
        other = (z_hi + d) % 4
        return other, (half * 16 + other * 4 + z_lo, col)

    def z_peer(d):
        other = (z + d) % 16
        return other, (half * 16 + other, col)

    barrier = pltpu.get_barrier_semaphore()

    def greet(device):
        pl.semaphore_signal(barrier, inc=1, device_id=device, device_id_type=MESH)

    def greet_source(t, carry):
        source = (t // 4) * 4 + core * 2 + (t // 2) % 2
        source_col = chip * 2 + t % 2

        @pl.when(jnp.logical_or(source != row, source_col != col))
        def _():
            greet((source, source_col))

        return carry

    lax.fori_loop(0, 32, greet_source, 0)

    def greet_plane(d, carry):
        greet(plane_peer(16 - d)[2])
        return carry

    def greet_z(d, carry):
        greet(z_peer(16 - d)[1])
        return carry

    lax.fori_loop(1, 16, greet_plane, 0)
    lax.fori_loop(1, 16, greet_z, 0)
    greet((row, chip * 2 + 1 - core))

    load_amp.wait()

    def pack(g, carry):
        lane = lax.broadcasted_iota(jnp.int32, (40, 128), 1)
        lane8 = lax.broadcasted_iota(jnp.int32, (8, 128), 1)
        sub8 = lax.broadcasted_iota(jnp.int32, (8, 128), 0)

        def load(t):
            return amp[:, pl.ds(pl.multiple_of(g * 1408 + t * 128, 128), 128)]

        for j in range(4):
            first, shift = (352 * j) // 128, (352 * j) % 128
            tiles = []
            for n in range(3):
                tile = load(first + n)
                if shift > 0:
                    tile = pltpu.roll(tile, 128 - shift, 1)
                    if first + n + 1 <= 10:
                        after = pltpu.roll(load(first + n + 1), 128 - shift, 1)
                        tile = jnp.where(lane < 128 - shift, tile, after)
                tiles.append(tile)
            dest = g * 4 + j
            for i in range(4):
                send_a[i, dest, 0] = tiles[0][8 * i:8 * i + 8]
                send_a[i, dest, 1] = tiles[1][8 * i:8 * i + 8]
                spare = pltpu.roll(tiles[2][32:40], 96 - 32 * i, 1) if i < 3 else jnp.zeros((8, 128), F32)
                send_a[i, dest, 2] = jnp.where(lane8 < 96, tiles[2][8 * i:8 * i + 8], spare)
            first8, second8 = tiles[0][32:40], tiles[1][32:40]
            send_b[0, dest] = jnp.where(sub8 < 4, first8, pltpu.roll(second8, 4, 0))
            send_b[1, dest] = jnp.where(sub8 < 4, pltpu.roll(first8, 4, 0), second8)
        return carry

    lax.fori_loop(0, 8, pack, 0)
    load_int.wait()

    copies = jnp.where(mine, 31, 32)
    pl.semaphore_wait(barrier, copies + 15 + 15 + 1)

    sibling = pltpu.make_async_remote_copy(
        ints.at[core], ints.at[core], int_sem.at[0], int_sem.at[1],
        device_id=(row, chip * 2 + 1 - core), device_id_type=MESH,
    )
    sibling.start()

    def outgoing(i):
        return send_a.at[i] if i < 4 else send_b.at[i - 4]

    def incoming(i):
        return recv_a.at[i] if i < 4 else recv_b.at[i - 4]

    def part(i):
        return part_a.at[i] if i < 4 else part_b.at[i - 4]

    def plane(i):
        return plane_a.at[i] if i < 4 else plane_b.at[i - 4]

    def near_out(i):
        return near_out_a.at[i] if i < 4 else near_out_b.at[i - 4]

    def send_round(i):
        src, dst = outgoing(i), incoming(i).at[core, slot]

        def send(t, carry):
            k = t // 2
            dz = jnp.where(k % 2 == 1, 8 - (k + 1) // 2, 8 + k // 2)
            other = ((half + t + 1) % 2) * 16 + (z + dz) % 16
            pltpu.make_async_remote_copy(
                src.at[other], dst, send_sem.at[i], recv_sem.at[i],
                device_id=(other, target), device_id_type=MESH,
            ).start()
            return carry

        lax.fori_loop(0, 31, send, 0)

        @pl.when(mine)
        def _():
            pltpu.make_async_copy(src.at[row], dst, recv_sem.at[i]).start()

        @pl.when(jnp.logical_not(mine))
        def _():
            pltpu.make_async_remote_copy(
                src.at[row], dst, send_sem.at[i], recv_sem.at[i],
                device_id=(row, target), device_id_type=MESH,
            ).start()

    for i in range(3):
        send_round(i)

    sibling.wait()
    for c in range(2):
        whole = ints[c]
        upper = whole.astype(BF16)
        hi[384 * c:384 * c + 352] = upper
        lo[384 * c:384 * c + 352] = (whole - upper.astype(F32)).astype(BF16)
        hi[384 * c + 352:384 * c + 384] = jnp.zeros((32, 768), BF16)
        lo[384 * c + 352:384 * c + 384] = jnp.zeros((32, 768), BF16)

    def gathered(i):
        if i < 4:
            return jnp.concatenate(
                [recv_a[i, c, :, n].reshape(128, 128) for c in range(2) for n in range(3)], axis=1
            )
        sub = lax.broadcasted_iota(jnp.int32, (64, 128), 0) % 8
        lane = lax.broadcasted_iota(jnp.int32, (64, 128), 1)

        def evens_odds(ref):
            whole = ref.reshape(8, 2, 8, 128)
            return whole[:, 0].reshape(64, 128), whole[:, 1].reshape(64, 128)

        def upper_rows(even, odd):
            return jnp.where(sub < 4, even, pltpu.roll(odd, 4, 0))

        def lower_rows(even, odd):
            return jnp.where(sub < 4, pltpu.roll(even, 60, 0), odd)

        parts = []
        for c in range(2):
            even, odd = evens_odds(recv_b[i - 4, c])
            parts += [upper_rows(even, odd), lower_rows(even, odd)]
            last = jnp.zeros((64, 128), F32)
            for g in range(3):
                even, odd = evens_odds(recv_a[g, c, :, 2])
                merged = upper_rows(even, odd) if i == 4 else lower_rows(even, odd)
                moved = pltpu.roll(merged, 32 + 32 * g, 1)
                last = jnp.where(jnp.logical_and(lane >= 32 * g, lane < 32 * g + 32), moved, last)
            parts.append(last)
        return jnp.concatenate(parts, axis=1)

    def product(i):
        left = gathered(i)
        upper = left.astype(BF16)
        lower = (left - upper.astype(F32)).astype(BF16)
        for h in range(2):
            lanes = slice(384 * h, 384 * h + 384)
            summed = jnp.dot(upper, lo[:, lanes], preferred_element_type=F32)
            summed += jnp.dot(lower, hi[:, lanes], preferred_element_type=F32)
            summed += jnp.dot(upper, hi[:, lanes], preferred_element_type=F32)
            part(i)[h] = summed.reshape(8, 16 if i < 4 else 8, 384)

    def send_plane(i):
        def send(d, carry):
            other_half, other_chip, device = plane_peer(d)
            pltpu.make_async_remote_copy(
                part(i).at[other_half, other_chip], plane(i).at[d - 1], plane_send.at[i], plane_recv.at[i],
                device_id=device, device_id_type=MESH,
            ).start()
            return carry

        lax.fori_loop(1, 16, send, 0)

    def sum_plane(i):
        wait_for(plane(i), plane_recv.at[i])
        summed = part(i)[half, chip]
        for d in range(15):
            summed = summed + plane(i)[d]
        rows = summed.shape[0]
        lane = lax.broadcasted_iota(jnp.int32, (rows, 128), 1)
        for low in range(4):
            spread = jnp.zeros((rows, 128), F32)
            for high in range(4):
                start = 24 * (4 * high + low)
                done = 0
                while done < 24:
                    tile, offset = (start + done) // 128, (start + done) % 128
                    count = min(24 - done, 128 - offset)
                    to = 32 * high + done
                    moved = summed[:, 128 * tile:128 * tile + 128]
                    if (to - offset) % 128:
                        moved = pltpu.roll(moved, (to - offset) % 128, 1)
                    spread = jnp.where(jnp.logical_and(lane >= to, lane < to + count), moved, spread)
                    done += count
            near_out(i)[low] = spread

    def send_near(i):
        for d in range(1, 4):
            other, device = near_peer(d)
            pltpu.make_async_remote_copy(
                near_out_a.at[i, other], near_in.at[i, d - 1], near_send.at[i, d - 1], near_recv.at[i, d - 1],
                device_id=device, device_id_type=MESH,
            ).start()

    def sum_near(i):
        summed = near_out_a[i, z_lo]
        for d in range(1, 4):
            wait_for(near_in.at[i, d - 1], near_recv.at[i, d - 1])
            summed = summed + near_in[i, d - 1]
        total[8 * i:8 * i + 8] = summed[0:8]
        total[40 + 8 * i:48 + 8 * i] = summed[8:16]

    def send_last(i):
        def send(d, carry):
            other, device = z_peer(d)
            pltpu.make_async_remote_copy(
                near_out_b.at[i - 4, other % 4], last_in.at[i - 4, d - 1], last_send.at[i - 4], last_recv.at[i - 4],
                device_id=device, device_id_type=MESH,
            ).start()
            return carry

        lax.fori_loop(1, 16, send, 0)

    def sum_last(i):
        wait_for(last_in.at[i - 4], last_recv.at[i - 4])
        summed = near_out_b[i - 4, z_lo]
        for d in range(15):
            summed = summed + last_in[i - 4, d]
        return summed

    for rows in (slice(32, 40), slice(72, 128)):
        total[rows] = jnp.zeros((rows.stop - rows.start, 128), F32)
    for i in range(ROUNDS):
        wait_for(incoming(i), recv_sem.at[i])
        if i + 3 < ROUNDS:
            send_round(i + 3)
        product(i)
        send_plane(i)
        if i >= 1:
            sum_plane(i - 1)
            if i <= 4:
                send_near(i - 1)
            else:
                send_last(i - 1)
        if i >= 2:
            sum_near(i - 2)

    far_out[...] = total[...].T.reshape(4, 32, 128)
    for d in range(1, 4):
        other, device = far_peer(d)
        pltpu.make_async_remote_copy(
            far_out.at[other, pl.ds(0, 24)], far_in.at[d - 1], far_send.at[d - 1], far_recv.at[d - 1],
            device_id=device, device_id_type=MESH,
        ).start()

    sum_plane(ROUNDS - 1)
    send_last(ROUNDS - 1)

    summed = far_out[z_hi, 0:24]
    for d in range(1, 4):
        wait_for(far_in.at[d - 1], far_recv.at[d - 1])
        summed = summed + far_in[d - 1]

    for rows in (slice(0, 32), slice(40, 72)):
        total[rows] = jnp.zeros((32, 128), F32)
    sub = lax.broadcasted_iota(jnp.int32, (8, 128), 0)
    fourth, fifth = sum_last(4), sum_last(5)
    total[32:40] = jnp.where(sub < 4, fourth, pltpu.roll(fifth, 4, 0))
    total[72:80] = jnp.where(sub < 4, pltpu.roll(fourth, 4, 0), fifth)
    turned[...] = total[...].T.reshape(4, 32, 128)
    out_ref[...] = (summed + turned[z_hi, 0:24])[:, 0:80]

    for i in range(ROUNDS):
        @pl.when(mine)
        def _():
            wait_for(outgoing(i).at[pl.ds(0, 31)], send_sem.at[i])

        @pl.when(jnp.logical_not(mine))
        def _():
            wait_for(outgoing(i), send_sem.at[i])

        wait_for(plane(i), plane_send.at[i])
        if i < 4:
            for d in range(3):
                wait_for(near_in.at[i, d], near_send.at[i, d])
        else:
            wait_for(last_in.at[i - 4], last_send.at[i - 4])
    for d in range(3):
        wait_for(far_in.at[d], far_send.at[d])


def per_device(amplitudes, integrals):
    flat = integrals.reshape(768, 352).T
    dma = pltpu.SemaphoreType.DMA
    return pl.pallas_call(
        kernel,
        out_shape=jax.ShapeDtypeStruct((24, 80), F32),
        in_specs=[pl.BlockSpec(memory_space=pl.ANY)] * 2,
        out_specs=pl.BlockSpec(memory_space=pltpu.VMEM),
        scratch_shapes=[
            pltpu.VMEM((40, 11264), F32),
            pltpu.VMEM((2, 352, 768), F32),
            pltpu.VMEM((768, 768), BF16),
            pltpu.VMEM((768, 768), BF16),
            pltpu.VMEM((4, 32, 3, 8, 128), F32),
            pltpu.VMEM((2, 32, 8, 128), F32),
            pltpu.VMEM((4, 2, 16, 3, 8, 128), F32),
            pltpu.VMEM((2, 2, 16, 8, 128), F32),
            pltpu.VMEM((4, 2, 8, 16, 384), F32),
            pltpu.VMEM((2, 2, 8, 8, 384), F32),
            pltpu.VMEM((4, 15, 16, 384), F32),
            pltpu.VMEM((2, 15, 8, 384), F32),
            pltpu.VMEM((4, 4, 16, 128), F32),
            pltpu.VMEM((2, 4, 8, 128), F32),
            pltpu.VMEM((4, 3, 16, 128), F32),
            pltpu.VMEM((128, 128), F32),
            pltpu.VMEM((4, 32, 128), F32),
            pltpu.VMEM((4, 32, 128), F32),
            pltpu.VMEM((3, 24, 128), F32),
            pltpu.VMEM((2, 15, 8, 128), F32),
            dma((2,)),
            dma((2,)),
            dma((ROUNDS,)),
            dma((ROUNDS,)),
            dma((ROUNDS,)),
            dma((ROUNDS,)),
            dma((4, 3)),
            dma((4, 3)),
            dma((3,)),
            dma((3,)),
            dma((2,)),
            dma((2,)),
        ],
        compiler_params=pltpu.CompilerParams(
            collective_id=0, has_side_effects=True, vmem_limit_bytes=60 << 20
        ),
    )(amplitudes, flat)


def solution(mesh):
    return jax.shard_map(
        per_device,
        mesh=mesh,
        in_specs=(P("row", "col"), P(None, "col", "row", None)),
        out_specs=P("row", "col"),
        check_vma=False,
    )
```
